32 devices in a mesh: fsdp: 8 (over z, y), seq: 4 (over x, core).
Axes of the slice: x: 2, y: 2, z: 4, core: 2. Of those that a mesh axis runs over, the one named last changes fastest.
Arguments:
- hidden_in: bfloat16 [32, 512, 768], P('fsdp', 'seq'), may hold values from -6 to 6
- encoder_states: bfloat16 [32, 256, 768], P('fsdp', 'seq'), may hold values from -6 to 6
- dec_segments: int32 [32, 512], P('fsdp', 'seq'), may hold values from 0 to 2, as said below
- enc_segments: int32 [32, 256], P('fsdp', 'seq'), may hold values from 0 to 2, as said below
- cotangent: bfloat16 [32, 512, 768], P('fsdp', 'seq'), may hold values from -6 to 6
- self_query: bfloat16 [768, 768], P(('fsdp', 'seq')), may hold values from -0.02734375 to 0.02734375
- self_key: bfloat16 [768, 768], P(('fsdp', 'seq')), may hold values from -0.21875 to 0.21875
- self_value: bfloat16 [768, 768], P(('fsdp', 'seq')), may hold values from -0.21875 to 0.21875
- self_output: bfloat16 [768, 768], P(('fsdp', 'seq')), may hold values from -0.875 to 0.875
- cross_query: bfloat16 [768, 768], P(('fsdp', 'seq')), may hold values from -0.02734375 to 0.02734375
- cross_key: bfloat16 [768, 768], P(('fsdp', 'seq')), may hold values from -0.21875 to 0.21875
- cross_value: bfloat16 [768, 768], P(('fsdp', 'seq')), may hold values from -0.21875 to 0.21875
- cross_output: bfloat16 [768, 768], P(('fsdp', 'seq')), may hold values from -0.875 to 0.875
- ffn_gate: bfloat16 [768, 2048], P(('fsdp', 'seq')), may hold values from -0.21875 to 0.21875
- ffn_up: bfloat16 [768, 2048], P(('fsdp', 'seq')), may hold values from -0.21875 to 0.21875
- ffn_down: bfloat16 [2048, 768], P(('fsdp', 'seq')), may hold values from -0.125 to 0.125
- norm_self: bfloat16 [768], P(('fsdp', 'seq')), may hold values from 0.5 to 1.5
- norm_cross: bfloat16 [768], P(('fsdp', 'seq')), may hold values from 0.5 to 1.5
- norm_ffn: bfloat16 [768], P(('fsdp', 'seq')), may hold values from 0.5 to 1.5
- bias_table: float32 [32, 12], P('seq'), may hold values from -4 to 4
Outputs:
- layer_out: bfloat16 [32, 512, 768], P('fsdp', 'seq')
- input_grad: bfloat16 [32, 512, 768], P('fsdp', 'seq')
- encoder_grad: bfloat16 [32, 256, 768], P('fsdp', 'seq')
- grad_self_query: float32 [768, 768], P(('fsdp', 'seq'))
- grad_self_key: float32 [768, 768], P(('fsdp', 'seq'))
- grad_self_value: float32 [768, 768], P(('fsdp', 'seq'))
- grad_self_output: float32 [768, 768], P(('fsdp', 'seq'))
- grad_cross_query: float32 [768, 768], P(('fsdp', 'seq'))
- grad_cross_key: float32 [768, 768], P(('fsdp', 'seq'))
- grad_cross_value: float32 [768, 768], P(('fsdp', 'seq'))
- grad_cross_output: float32 [768, 768], P(('fsdp', 'seq'))
- grad_ffn_gate: float32 [768, 2048], P(('fsdp', 'seq'))
- grad_ffn_up: float32 [768, 2048], P(('fsdp', 'seq'))
- grad_ffn_down: float32 [2048, 768], P(('fsdp', 'seq'))
- grad_norm_self: float32 [768], P(('fsdp', 'seq'))
- grad_norm_cross: float32 [768], P(('fsdp', 'seq'))
- grad_norm_ffn: float32 [768], P(('fsdp', 'seq'))
- grad_bias_table: float32 [32, 12], P('seq')
The draws below stay inside these ranges and needn't reach their ends.
Inputs may be any that keep to these rules, and one draw needn't show every extreme that they name: `dec_segments`: along each row the numbers start at 0 and never fall; a row's decoder positions and its encoder states use the same set of numbers; in each aligned block of 4 rows one row holds a single document. `enc_segments`: along each row the numbers start at 0 and never fall, with the same set as the row's decoder positions.
All inputs are finite; a program needn't handle non-finite values.
Results may differ from the reference program's by a relative error of at most 0.023.
Values may be sent and summed in bfloat16 or wider, within the bound.
A program may use at most 192 MiB of HBM per device.

```python
import jax
import jax.numpy as jnp
from jax import lax

D = 768
H = 12
DH = 64
FF = 2048
NB = 32
LEN = 512
ENC = 256
ROWS_DEV = 4
ROWS = 32


def segment_plan(key):
    keys_all = jax.random.split(key, 6)
    counts = jax.random.randint(keys_all[0], (ROWS,), 0, 3)
    blocks = ROWS // ROWS_DEV
    whole_row = jax.random.randint(keys_all[1], (blocks,), 0, ROWS_DEV)
    row_index = jnp.arange(ROWS)
    chosen = jnp.repeat(whole_row, ROWS_DEV) + row_index // ROWS_DEV * ROWS_DEV
    counts = jnp.where(row_index == chosen, 0, counts)
    counts = jnp.where(row_index == (whole_row[0] + 1) % ROWS_DEV, 2, counts)
    first_cut = jax.random.randint(keys_all[2], (ROWS,), 1, LEN // 2)
    second_cut = jax.random.randint(keys_all[3], (ROWS,), LEN // 2, LEN)
    first_enc = jax.random.randint(keys_all[4], (ROWS,), 1, ENC // 2)
    second_enc = jax.random.randint(keys_all[5], (ROWS,), ENC // 2, ENC)
    return (counts, first_cut, second_cut, first_enc, second_enc)


def number_segments(length, counts, first_cut, second_cut):
    positions = jnp.arange(length)[None, :]
    past_first = (positions >= first_cut[:, None]) & (counts[:, None] >= 1)
    past_second = (positions >= second_cut[:, None]) & (counts[:, None] >= 2)
    return past_first.astype(jnp.int32) + past_second.astype(jnp.int32)


def draw_dec_segments(key, part):
    counts, first_cut, second_cut, first_enc, second_enc = segment_plan(key)
    return number_segments(LEN, counts, first_cut, second_cut)


def draw_enc_segments(key, part):
    counts, first_cut, second_cut, first_enc, second_enc = segment_plan(key)
    return number_segments(ENC, counts, first_enc, second_enc)


def steps_of(rng, extent, shards, low, high):
    def one(dim, blocks):
        draws = jax.random.uniform(jax.random.fold_in(jax.random.fold_in(rng, 6), dim), (blocks,), jnp.float32, low / len(shards), high / len(shards))
        return jnp.repeat(jnp.exp(draws), extent[dim] // blocks).reshape((-1,) + (1,) * (len(extent) - dim - 1))

    level = one(*shards[0])
    for cut in shards[1:]:
        level = level * one(*cut)
    return level


def bell_draw(key, shape, deviation, most, shards=(), kind=jnp.bfloat16):
    factor_of = steps_of(key, shape, shards, -0.22, 0.18) if shards else 1.0
    values = jax.random.normal(key, shape, jnp.float32) * deviation * factor_of
    return jnp.minimum(jnp.maximum(values, -most), most).astype(kind)


def setup_inputs(seed: int = 0) -> dict:
    keys = jax.random.split(jax.random.key(seed), 21)
    hidden_in = bell_draw(keys[0], (ROWS, LEN, D), 1.0, 6.0, ((0, 8), (1, 4)))
    encoder_states = bell_draw(keys[1], (ROWS, ENC, D), 1.0, 6.0, ((0, 8), (1, 4)))
    dec_segments = draw_dec_segments(jax.random.fold_in(keys[20], 71), 0)
    enc_segments = draw_enc_segments(jax.random.fold_in(keys[20], 71), 0)
    cotangent = bell_draw(keys[4], (ROWS, LEN, D), 1.0, 6.0, ((0, 8), (1, 4)))
    self_query = bell_draw(keys[5], (D, D), (D * DH) ** -0.5, 0.02734375, ((0, 32),))
    self_key = bell_draw(keys[6], (D, D), D ** -0.5, 0.21875, ((0, 32),))
    self_value = bell_draw(keys[7], (D, D), D ** -0.5, 0.21875, ((0, 32),))
    self_output = bell_draw(keys[8], (D, D), (D // 16) ** -0.5, 0.875, ((0, 32),))
    cross_query = bell_draw(keys[9], (D, D), (D * DH) ** -0.5, 0.02734375, ((0, 32),))
    cross_key = bell_draw(keys[10], (D, D), D ** -0.5, 0.21875, ((0, 32),))
    cross_value = bell_draw(keys[11], (D, D), D ** -0.5, 0.21875, ((0, 32),))
    cross_output = bell_draw(keys[12], (D, D), (D // 16) ** -0.5, 0.875, ((0, 32),))
    ffn_gate = bell_draw(keys[13], (D, FF), D ** -0.5, 0.21875, ((0, 32),))
    ffn_up = bell_draw(keys[14], (D, FF), D ** -0.5, 0.21875, ((0, 32),))
    ffn_down = bell_draw(keys[15], (FF, D), FF ** -0.5, 0.125, ((0, 32),))
    norm_self = jnp.clip(1.0 + 0.1 * jax.random.normal(keys[16], (D,), jnp.float32), 0.5, 1.5).astype(jnp.bfloat16)
    norm_cross = jnp.clip(1.0 + 0.1 * jax.random.normal(keys[17], (D,), jnp.float32), 0.5, 1.5).astype(jnp.bfloat16)
    norm_ffn = jnp.clip(1.0 + 0.1 * jax.random.normal(keys[18], (D,), jnp.float32), 0.5, 1.5).astype(jnp.bfloat16)
    bias_table = bell_draw(keys[19], (NB, H), 1.0, 4.0, ((0, 4),), jnp.float32)
    return dict(hidden_in=hidden_in, encoder_states=encoder_states, dec_segments=dec_segments, enc_segments=enc_segments, cotangent=cotangent, self_query=self_query, self_key=self_key, self_value=self_value, self_output=self_output, cross_query=cross_query, cross_key=cross_key, cross_value=cross_value, cross_output=cross_output, ffn_gate=ffn_gate, ffn_up=ffn_up, ffn_down=ffn_down, norm_self=norm_self, norm_cross=norm_cross, norm_ffn=norm_ffn, bias_table=bias_table)


EPS = 1e-06
NEG_LARGE = -1000000000.0
HIGH = lax.Precision.HIGHEST
THRESHOLDS = (19, 21, 24, 27, 31, 35, 40, 46, 52, 59, 67, 77, 87, 99, 113)

@jax.custom_vjp
def low(v):
    return lax.optimization_barrier(v.astype(jnp.bfloat16)).astype(jnp.float32)

@jax.custom_vjp
def low_back(v):
    return v

def low_keep(v):
    return (low(v), None)

def low_pass(kept, grad):
    return (grad,)

def back_keep(v):
    return (v, None)

def back_low(kept, grad):
    return (low(grad),)
low.defvjp(low_keep, low_pass)
low_back.defvjp(back_keep, back_low)

def buckets(query_pos, key_pos):
    distance = jnp.maximum(query_pos[:, None] - key_pos[None, :], 0)
    result = jnp.minimum(distance, 16)
    for threshold in THRESHOLDS:
        result = result + (distance >= threshold).astype(jnp.int32)
    return result

def rms_norm(values, gain_vec):
    return values * lax.rsqrt(lax.optimization_barrier(jnp.mean(values * values, axis=-1, keepdims=True)) + EPS) * gain_vec

def project(values, weight):
    return jnp.einsum('rtd,de->rte', values, weight, precision=HIGH)

def attend(queries, key_rows, value_rows, allowed, pos_bias):
    scores = jnp.einsum('qhd,khd->hqk', queries, key_rows, precision=HIGH) + pos_bias
    scores = low_back(scores)
    scores = jnp.where(allowed[None], scores, NEG_LARGE)
    attn_probs = low(jax.nn.softmax(scores, axis=-1))
    return jnp.einsum('hqk,khd->qhd', attn_probs, value_rows, precision=HIGH)

def decoder_layer(params, hidden_in, encoder, dec_seg, enc_seg):
    self_query, self_key, self_value, self_output, cross_query, cross_key, cross_value, cross_output, ffn_gate, ffn_up, ffn_down, norm_self, norm_cross, norm_ffn, bias_table = params
    row_count = hidden_in.shape[0]
    positions = jnp.arange(LEN)
    pos_bias = jnp.transpose(bias_table[buckets(positions, positions)], (2, 0, 1))
    causal = positions[:, None] >= positions[None, :]

    def split_heads(values, length):
        return values.reshape(row_count, length, H, DH)
    normed = low(rms_norm(hidden_in, norm_self))
    queries = split_heads(low(low_back(project(normed, self_query))), LEN)
    key_rows = split_heads(low(low_back(project(normed, self_key))), LEN)
    value_rows = split_heads(low(low_back(project(normed, self_value))), LEN)

    def self_row(row_items):
        row_query, row_key, row_value, row_seg = row_items
        allowed = causal & (row_seg[:, None] == row_seg[None, :])
        return attend(row_query, row_key, row_value, allowed, pos_bias)
    mixed_self = lax.map(jax.checkpoint(self_row), (queries, key_rows, value_rows, dec_seg))
    attn_self = low(low_back(mixed_self.reshape(row_count, LEN, D)))
    after_self = hidden_in + low_back(project(attn_self, self_output))
    normed_cross = low(rms_norm(after_self, norm_cross))
    cross_q = split_heads(low(low_back(project(normed_cross, cross_query))), LEN)
    cross_k = split_heads(low(low_back(project(encoder, cross_key))), ENC)
    cross_v = split_heads(low(low_back(project(encoder, cross_value))), ENC)

    def cross_row(row_items):
        row_query, row_key, row_value, row_seg, row_enc = row_items
        allowed = row_seg[:, None] == row_enc[None, :]
        return attend(row_query, row_key, row_value, allowed, 0.0)
    mixed_cross = lax.map(jax.checkpoint(cross_row), (cross_q, cross_k, cross_v, dec_seg, enc_seg))
    attn_cross = low(low_back(mixed_cross.reshape(row_count, LEN, D)))
    after_cross = after_self + low_back(project(attn_cross, cross_output))
    normed_ffn = low(rms_norm(after_cross, norm_ffn))
    gate_pre = low_back(project(normed_ffn, ffn_gate))
    up_pre = low_back(project(normed_ffn, ffn_up))
    hidden_units = low(jax.nn.gelu(gate_pre, approximate=True) * up_pre)
    return after_cross + low_back(project(hidden_units, ffn_down))

def reference(hidden_in, encoder_states, dec_segments, enc_segments, cotangent, self_query, self_key, self_value, self_output, cross_query, cross_key, cross_value, cross_output, ffn_gate, ffn_up, ffn_down, norm_self, norm_cross, norm_ffn, bias_table):
    params = tuple((weight_arr.astype(jnp.float32) for weight_arr in (self_query, self_key, self_value, self_output, cross_query, cross_key, cross_value, cross_output, ffn_gate, ffn_up, ffn_down, norm_self, norm_cross, norm_ffn, bias_table)))
    group = ROWS_DEV
    blocks = ROWS // group

    def regroup(array_in):
        return array_in.reshape((blocks, group) + array_in.shape[1:])

    def step(totals, block_items):
        hidden_blk, encoder_blk, dec_blk, enc_blk, cot_blk = block_items

        def inner(weights_all, hidden_vals, encoder_vals):
            return decoder_layer(weights_all, hidden_vals, encoder_vals, dec_blk, enc_blk)
        out_vals, pull = jax.vjp(inner, params, hidden_blk.astype(jnp.float32), encoder_blk.astype(jnp.float32))
        grad_params, grad_hidden, grad_encoder = pull(cot_blk.astype(jnp.float32))
        totals = jax.tree.map(lambda acc_val, new_val: acc_val + new_val, totals, grad_params)
        return (totals, (out_vals.astype(jnp.bfloat16), grad_hidden.astype(jnp.bfloat16), grad_encoder.astype(jnp.bfloat16)))
    zeros_init = jax.tree.map(jnp.zeros_like, params)
    totals, (out_blocks, grad_blocks, enc_blocks) = lax.scan(step, zeros_init, (regroup(hidden_in), regroup(encoder_states), regroup(dec_segments), regroup(enc_segments), regroup(cotangent)))
    layer_out = out_blocks.reshape(ROWS, LEN, D)
    input_grad = grad_blocks.reshape(ROWS, LEN, D)
    encoder_grad = enc_blocks.reshape(ROWS, ENC, D)
    return (layer_out, input_grad, encoder_grad, totals[0], totals[1], totals[2], totals[3], totals[4], totals[5], totals[6], totals[7], totals[8], totals[9], totals[10], totals[11], totals[12], totals[13], totals[14])
```

```python
from functools import partial
import math

import jax
import jax.numpy as jnp
from jax import lax
from jax.sharding import PartitionSpec as P

DH = 64
NB = 32


EPS = 1e-06
NEG_LARGE = -1000000000.0
HIGH = lax.Precision.HIGHEST
THRESHOLDS = (19, 21, 24, 27, 31, 35, 40, 46, 52, 59, 67, 77, 87, 99, 113)


def matmul(left, right):
    return jnp.dot(left, right, preferred_element_type=jnp.float32)


def matmul_left_t(left, right):
    return lax.dot_general(
        left, right, (((0,), (0,)), ((), ())), preferred_element_type=jnp.float32
    )


def matmul_right_t(left, right):
    return lax.dot_general(
        left, right, (((1,), (1,)), ((), ())), preferred_element_type=jnp.float32
    )


def bucket_table(query_pos, key_pos):
    distance = jnp.maximum(query_pos[:, None] - key_pos[None, :], 0)
    bucket_ids = jnp.minimum(distance, 16)
    for threshold in THRESHOLDS:
        bucket_ids = bucket_ids + (distance >= threshold).astype(jnp.int32)
    return (bucket_ids[None] == jnp.arange(NB)[:, None, None]).astype(jnp.float32)


def norm_forward(values, gain_vec):
    scale = lax.rsqrt(jnp.mean(values * values, axis=-1, keepdims=True) + EPS)
    unit = values * scale
    return ((unit * gain_vec).astype(jnp.bfloat16), unit, scale)


def norm_backward(grad_normed, unit, scale, gain_vec):
    grad_unit = grad_normed * gain_vec
    grad_gain = jnp.sum(grad_normed * unit, axis=0)
    grad_values = scale * (grad_unit - unit * jnp.mean(grad_unit * unit, axis=-1, keepdims=True))
    return (grad_values, grad_gain)


def attn_scores(queries, key_rows, allowed, pos_bias):
    scores = (
        jnp.einsum("bqhd,bkhd->bhqk", queries, key_rows, preferred_element_type=jnp.float32)
        + pos_bias
    )
    return jnp.where(allowed[:, None], scores, NEG_LARGE)


def attn_forward(queries, key_rows, value_rows, allowed, pos_bias):
    scores = attn_scores(queries, key_rows, allowed, pos_bias)
    top_score = jnp.max(scores, axis=-1, keepdims=True)
    expo = jnp.exp(scores - top_score)
    total = jnp.sum(expo, axis=-1, keepdims=True)
    attn_probs = (expo / total).astype(jnp.bfloat16)
    mixed = jnp.einsum(
        "bhqk,bkhd->bqhd", attn_probs, value_rows, preferred_element_type=jnp.float32
    )
    return (mixed, top_score + jnp.log(total))


def attn_query_side(queries, key_rows, value_rows, allowed, pos_bias, log_total, grad_mixed):
    scores = attn_scores(queries, key_rows, allowed, pos_bias)
    attn_probs = jnp.exp(scores - log_total)
    grad_probs = jnp.einsum(
        "bqhd,bkhd->bhqk", grad_mixed, value_rows, preferred_element_type=jnp.float32
    )
    row_stat = jnp.sum(grad_probs * attn_probs, axis=-1, keepdims=True)
    grad_scores = attn_probs * (grad_probs - row_stat)
    grad_low = grad_scores.astype(jnp.bfloat16)
    grad_query = jnp.einsum(
        "bhqk,bkhd->bqhd", grad_low, key_rows, preferred_element_type=jnp.float32
    )
    return (grad_query, grad_low, attn_probs, row_stat)


def attn_backward(queries, key_rows, value_rows, allowed, pos_bias, log_total, grad_mixed):
    grad_query, grad_low, attn_probs, row_stat = attn_query_side(
        queries, key_rows, value_rows, allowed, pos_bias, log_total, grad_mixed
    )
    grad_key = jnp.einsum("bhqk,bqhd->bkhd", grad_low, queries, preferred_element_type=jnp.float32)
    grad_value = jnp.einsum(
        "bhqk,bqhd->bkhd",
        attn_probs.astype(jnp.bfloat16),
        grad_mixed,
        preferred_element_type=jnp.float32,
    )
    return (grad_query, grad_key, grad_value, grad_low)


def per_device(
    hidden_in,
    encoder_states,
    dec_segments,
    enc_segments,
    cotangent,
    self_query,
    self_key,
    self_value,
    self_output,
    cross_query,
    cross_key,
    cross_value,
    cross_output,
    ffn_gate,
    ffn_up,
    ffn_down,
    norm_self,
    norm_cross,
    norm_ffn,
    bias_table,
):
    row_count, local_len, model_width = hidden_in.shape
    enc_local = encoder_states.shape[1]
    seq_size = lax.axis_size("seq")
    full_len = local_len * seq_size
    full_enc = enc_local * seq_size
    head_count = model_width // DH
    tokens = row_count * local_len
    axes = ("fsdp", "seq")
    total_devices = lax.axis_size("fsdp") * seq_size
    shard_rows = self_query.shape[0]
    down_rows, hidden_width = ffn_down.shape[0], ffn_gate.shape[1]
    folds = -(-down_rows // shard_rows)
    down_padded = jnp.pad(ffn_down, ((0, folds * shard_rows - down_rows), (0, 0)))
    gains = jnp.pad(jnp.stack([norm_self, norm_cross, norm_ffn], axis=1), ((0, 0), (0, 125)))
    first_pack = jnp.concatenate([self_query, self_key, self_value, gains], axis=1)
    rest_pack = jnp.concatenate(
        [self_output, cross_query, cross_key, cross_value, cross_output, ffn_gate, ffn_up]
        + [down_padded[i * shard_rows : (i + 1) * shard_rows] for i in range(folds)],
        axis=1,
    )
    first_full = lax.all_gather(first_pack, axes, axis=0, tiled=True)
    w_qkv = first_full[:, : 3 * model_width]
    gain_rows = first_full[:, 3 * model_width : 3 * model_width + 3].astype(jnp.float32)
    g_self, g_cross, g_ffn = gain_rows[:, 0], gain_rows[:, 1], gain_rows[:, 2]
    buckets_local = bias_table.shape[0]
    bias_high = bias_table.astype(jnp.bfloat16)
    bias_low = (bias_table - bias_high.astype(jnp.float32)).astype(jnp.bfloat16)
    bias_size = buckets_local * head_count
    side_parts = jnp.concatenate(
        [
            dec_segments.astype(jnp.bfloat16),
            enc_segments.astype(jnp.bfloat16),
            jnp.broadcast_to(bias_high.reshape(1, bias_size), (row_count, bias_size)),
            jnp.broadcast_to(bias_low.reshape(1, bias_size), (row_count, bias_size)),
        ],
        axis=1,
    )
    side_pad = jnp.pad(side_parts, ((0, 0), (0, model_width - side_parts.shape[1])))
    side_block = jnp.pad(side_pad[:, None, :], ((0, 0), (0, 15), (0, 0)))
    states_pack = jnp.concatenate([encoder_states, side_block], axis=1)
    states_gathered = lax.all_gather(states_pack, "seq", axis=1, tiled=False)
    states_full = states_gathered[:, :, :enc_local].reshape(row_count, full_enc, model_width)
    side_full = states_gathered[:, :, enc_local].astype(jnp.float32)
    seg_rows = side_full[:, :, :local_len].reshape(row_count, full_len).astype(jnp.int32)
    side_at = local_len + enc_local
    enc_rows = side_full[:, :, local_len:side_at].reshape(row_count, full_enc).astype(jnp.int32)
    table_full = (
        side_full[0, :, side_at : side_at + bias_size]
        + side_full[0, :, side_at + bias_size : side_at + 2 * bias_size]
    ).reshape(seq_size * buckets_local, head_count)
    rest_full = lax.all_gather(rest_pack, axes, axis=0, tiled=True)
    cuts = [model_width] * 5 + [hidden_width] * 2
    pieces, at = [], 0
    for width in cuts:
        pieces.append(rest_full[:, at : at + width])
        at += width
    w_out_self, c_query_w, c_key_w, c_value_w, c_out_w, f_gate, f_up = pieces
    down_folds = rest_full[:, at:].reshape(total_devices, shard_rows, folds, model_width)
    f_down = jnp.concatenate(
        [
            down_folds[:, : min(shard_rows, down_rows - i * shard_rows), i]
            for i in range(folds)
        ],
        axis=1,
    ).reshape(total_devices * down_rows, model_width)
    query_pos = lax.axis_index("seq") * local_len + jnp.arange(local_len)
    key_pos = jnp.arange(full_len)
    one_hot = bucket_table(query_pos, key_pos)
    pos_bias = jnp.einsum("nqk,nh->hqk", one_hot, table_full, precision=HIGH)
    causal = query_pos[:, None] >= key_pos[None, :]
    block_rows = math.gcd(row_count, max(1, 512 // local_len))
    blocks = row_count // block_rows

    def to_blocks(array_in):
        return array_in.reshape((blocks, block_rows) + array_in.shape[1:])

    x_flat = hidden_in.reshape(tokens, model_width).astype(jnp.float32)
    normed_self, unit_self, scale_self = norm_forward(x_flat, g_self)
    qkv_self = matmul(normed_self, w_qkv).astype(jnp.bfloat16)
    query_self = qkv_self[:, :model_width]
    key_self = qkv_self[:, model_width : 2 * model_width]
    value_self = qkv_self[:, 2 * model_width :]
    pair_self = jnp.stack([key_self, value_self]).reshape(2, row_count, local_len, model_width)
    pair_full = lax.all_gather(pair_self, "seq", axis=2, tiled=True)
    keys_full = pair_full[0].reshape(row_count, full_len, head_count, DH)
    values_full = pair_full[1].reshape(row_count, full_len, head_count, DH)
    queries_heads = query_self.reshape(row_count, local_len, head_count, DH)
    self_allowed = causal[None] & (dec_segments[:, :, None] == seg_rows[:, None, :])

    def self_forward(block_items):
        block_query, block_key, block_value, block_allowed = block_items
        return attn_forward(block_query, block_key, block_value, block_allowed, pos_bias)

    mixed_self, lse_self = lax.map(
        self_forward,
        (
            to_blocks(queries_heads),
            to_blocks(keys_full),
            to_blocks(values_full),
            to_blocks(self_allowed),
        ),
    )
    attn_self = mixed_self.reshape(tokens, model_width).astype(jnp.bfloat16)
    after_self = x_flat + matmul(attn_self, w_out_self)
    normed_cross, unit_cross, scale_cross = norm_forward(after_self, g_cross)
    query_cross = matmul(normed_cross, c_query_w).astype(jnp.bfloat16)
    states_flat = states_full.reshape(row_count * full_enc, model_width)
    key_cross = (
        matmul(states_flat, c_key_w)
        .astype(jnp.bfloat16)
        .reshape(row_count, full_enc, head_count, DH)
    )
    value_cross = (
        matmul(states_flat, c_value_w)
        .astype(jnp.bfloat16)
        .reshape(row_count, full_enc, head_count, DH)
    )
    cross_heads = query_cross.reshape(row_count, local_len, head_count, DH)
    cross_allowed = dec_segments[:, :, None] == enc_rows[:, None, :]

    def cross_forward(block_items):
        block_query, block_key, block_value, block_allowed = block_items
        return attn_forward(block_query, block_key, block_value, block_allowed, 0.0)

    mixed_cross, lse_cross = lax.map(
        cross_forward,
        (
            to_blocks(cross_heads),
            to_blocks(key_cross),
            to_blocks(value_cross),
            to_blocks(cross_allowed),
        ),
    )
    attn_cross = mixed_cross.reshape(tokens, model_width).astype(jnp.bfloat16)
    after_cross = after_self + matmul(attn_cross, c_out_w)
    normed_ffn, unit_ffn, scale_ffn = norm_forward(after_cross, g_ffn)
    gate_pre = matmul(normed_ffn, f_gate)
    up_pre = matmul(normed_ffn, f_up)
    gate_act = jax.nn.gelu(gate_pre, approximate=True)
    hidden_units = (gate_act * up_pre).astype(jnp.bfloat16)
    layer_out = after_cross + matmul(hidden_units, f_down)
    grad_top = cotangent.reshape(tokens, model_width).astype(jnp.float32)
    grad_top_low = grad_top.astype(jnp.bfloat16)
    grad_down_w = matmul_left_t(hidden_units, grad_top_low)
    grad_hidden = matmul_right_t(grad_top_low, f_down)
    gelu_value, gelu_pull = jax.vjp(partial(jax.nn.gelu, approximate=True), gate_pre)
    grad_gate = gelu_pull(grad_hidden * up_pre)[0].astype(jnp.bfloat16)
    grad_up = (grad_hidden * gate_act).astype(jnp.bfloat16)
    grad_gate_w = matmul_left_t(normed_ffn, grad_gate)
    grad_up_w = matmul_left_t(normed_ffn, grad_up)
    down_split = grad_down_w.astype(jnp.bfloat16).reshape(total_devices, down_rows, model_width)
    down_split = jnp.pad(down_split, ((0, 0), (0, folds * shard_rows - down_rows), (0, 0)))
    ffn_pack = jnp.concatenate(
        [grad_gate_w.astype(jnp.bfloat16), grad_up_w.astype(jnp.bfloat16)]
        + [
            down_split[:, i * shard_rows : (i + 1) * shard_rows].reshape(model_width, model_width)
            for i in range(folds)
        ],
        axis=1,
    )
    ffn_summed = lax.psum_scatter(ffn_pack, axes, scatter_dimension=0, tiled=True)
    ffn_summed = ffn_summed.astype(jnp.float32)
    down_share = jnp.concatenate(
        [
            ffn_summed[:, 2 * hidden_width + i * model_width :][:, :model_width]
            for i in range(folds)
        ],
        axis=0,
    )[:down_rows]
    grad_normed_ffn = matmul_right_t(grad_gate, f_gate) + matmul_right_t(grad_up, f_up)
    grad_res_ffn, grad_g_ffn = norm_backward(grad_normed_ffn, unit_ffn, scale_ffn, g_ffn)
    grad_after_cross = grad_top + grad_res_ffn
    grad_cross_low = grad_after_cross.astype(jnp.bfloat16)
    grad_c_out = matmul_left_t(attn_cross, grad_cross_low)
    grad_attn_cross = (
        matmul_right_t(grad_cross_low, c_out_w)
        .astype(jnp.bfloat16)
        .reshape(row_count, local_len, head_count, DH)
    )

    def cross_back(block_items):
        block_query, block_key, block_value, block_allowed, block_lse, block_grad = block_items
        grad_query, grad_key, grad_value, grad_low = attn_backward(
            block_query, block_key, block_value, block_allowed, 0.0, block_lse, block_grad
        )
        return (grad_query, grad_key, grad_value)

    grad_qc, grad_kc, grad_vc = lax.map(
        cross_back,
        (
            to_blocks(cross_heads),
            to_blocks(key_cross),
            to_blocks(value_cross),
            to_blocks(cross_allowed),
            lse_cross,
            to_blocks(grad_attn_cross),
        ),
    )
    grad_pair_cross = jnp.stack(
        [
            grad_kc.reshape(row_count, full_enc, model_width),
            grad_vc.reshape(row_count, full_enc, model_width),
        ]
    )
    summed_cross = lax.psum_scatter(
        grad_pair_cross.astype(jnp.bfloat16), "seq", scatter_dimension=2, tiled=True
    ).astype(jnp.float32)
    grad_kc_low = summed_cross[0].reshape(row_count * enc_local, model_width).astype(jnp.bfloat16)
    grad_vc_low = summed_cross[1].reshape(row_count * enc_local, model_width).astype(jnp.bfloat16)
    states_local = encoder_states.reshape(row_count * enc_local, model_width)
    grad_c_key = matmul_left_t(states_local, grad_kc_low)
    grad_c_value = matmul_left_t(states_local, grad_vc_low)
    grad_states = matmul_right_t(grad_kc_low, c_key_w) + matmul_right_t(grad_vc_low, c_value_w)
    grad_qc_low = grad_qc.reshape(tokens, model_width).astype(jnp.bfloat16)
    grad_c_query = matmul_left_t(normed_cross, grad_qc_low)
    grad_normed_cross = matmul_right_t(grad_qc_low, c_query_w)
    grad_res_cross, grad_g_cross = norm_backward(
        grad_normed_cross, unit_cross, scale_cross, g_cross
    )
    grad_after_self = grad_after_cross + grad_res_cross
    grad_self_low = grad_after_self.astype(jnp.bfloat16)
    grad_out_self_w = matmul_left_t(attn_self, grad_self_low)
    grad_attn_self = (
        matmul_right_t(grad_self_low, w_out_self)
        .astype(jnp.bfloat16)
        .reshape(row_count, local_len, head_count, DH)
    )

    def self_back(block_items):
        block_query, block_key, block_value, block_allowed, block_lse, block_grad = block_items
        grad_query, grad_key, grad_value, grad_low = attn_backward(
            block_query, block_key, block_value, block_allowed, pos_bias, block_lse, block_grad
        )
        bias_part = jnp.einsum(
            "hqk,nqk->nh", jnp.sum(grad_low.astype(jnp.float32), axis=0), one_hot, precision=HIGH
        )
        return (grad_query, grad_key, grad_value, bias_part)

    grad_qs, grad_ks, grad_vs, bias_parts = lax.map(
        self_back,
        (
            to_blocks(queries_heads),
            to_blocks(keys_full),
            to_blocks(values_full),
            to_blocks(self_allowed),
            lse_self,
            to_blocks(grad_attn_self),
        ),
    )
    grad_pair_self = jnp.stack(
        [
            grad_ks.reshape(row_count, full_len, model_width),
            grad_vs.reshape(row_count, full_len, model_width),
        ]
    )
    summed_self = lax.psum_scatter(
        grad_pair_self.astype(jnp.bfloat16), "seq", scatter_dimension=2, tiled=True
    ).astype(jnp.float32)
    grad_key_low = summed_self[0].reshape(tokens, model_width).astype(jnp.bfloat16)
    grad_value_low = summed_self[1].reshape(tokens, model_width).astype(jnp.bfloat16)
    grad_query_low = grad_qs.reshape(tokens, model_width).astype(jnp.bfloat16)
    grad_q_w = matmul_left_t(normed_self, grad_query_low)
    grad_k_w = matmul_left_t(normed_self, grad_key_low)
    grad_v_w = matmul_left_t(normed_self, grad_value_low)
    grad_normed_self = matmul_right_t(
        jnp.concatenate([grad_query_low, grad_key_low, grad_value_low], axis=1), w_qkv
    )
    grad_res_self, grad_g_self = norm_backward(grad_normed_self, unit_self, scale_self, g_self)
    grad_input = grad_after_self + grad_res_self
    bias_total = jnp.sum(bias_parts, axis=0)
    bias_columns = -(-bias_size // shard_rows)
    bias_spread = jnp.pad(
        bias_total.reshape(seq_size, bias_size),
        ((0, 0), (0, bias_columns * shard_rows - bias_size)),
    ).reshape(1, seq_size * shard_rows, bias_columns)
    fsdp_size = lax.axis_size("fsdp")
    bias_spread = jnp.broadcast_to(
        bias_spread, (fsdp_size, seq_size * shard_rows, bias_columns)
    ).reshape(model_width, bias_columns)
    small = jnp.concatenate(
        [jnp.stack([grad_g_self, grad_g_cross, grad_g_ffn], axis=1), bias_spread], axis=1
    )
    small = jnp.pad(small, ((0, 0), (0, 256 - small.shape[1])))
    late_pack = jnp.concatenate(
        [
            part.astype(jnp.bfloat16)
            for part in (
                grad_q_w,
                grad_k_w,
                grad_v_w,
                grad_out_self_w,
                grad_c_query,
                grad_c_key,
                grad_c_value,
                grad_c_out,
                small,
            )
        ],
        axis=1,
    )
    late_summed = lax.psum_scatter(late_pack, axes, scatter_dimension=0, tiled=True)
    late_summed = late_summed.astype(jnp.float32)
    small_summed = late_summed[:, 8 * model_width :]
    bias_sum = small_summed[:, 3 : 3 + bias_columns].reshape(-1)[:bias_size]
    bias_grad = bias_sum.reshape(buckets_local, head_count)
    grads_sharded = (
        *(late_summed[:, i * model_width : (i + 1) * model_width] for i in range(8)),
        ffn_summed[:, :hidden_width],
        ffn_summed[:, hidden_width : 2 * hidden_width],
        down_share,
        small_summed[:, 0],
        small_summed[:, 1],
        small_summed[:, 2],
    )
    return (
        layer_out.reshape(row_count, local_len, model_width).astype(jnp.bfloat16),
        grad_input.reshape(row_count, local_len, model_width).astype(jnp.bfloat16),
        grad_states.reshape(row_count, enc_local, model_width).astype(jnp.bfloat16),
        grads_sharded[0],
        grads_sharded[1],
        grads_sharded[2],
        grads_sharded[3],
        grads_sharded[4],
        grads_sharded[5],
        grads_sharded[6],
        grads_sharded[7],
        grads_sharded[8],
        grads_sharded[9],
        grads_sharded[10],
        grads_sharded[11],
        grads_sharded[12],
        grads_sharded[13],
        bias_grad,
    )


def solution(mesh):
    return jax.shard_map(
        per_device,
        mesh=mesh,
        in_specs=(
            P("fsdp", "seq", None),
            P("fsdp", "seq", None),
            P("fsdp", "seq"),
            P("fsdp", "seq"),
            P("fsdp", "seq", None),
            P(("fsdp", "seq"), None),
            P(("fsdp", "seq"), None),
            P(("fsdp", "seq"), None),
            P(("fsdp", "seq"), None),
            P(("fsdp", "seq"), None),
            P(("fsdp", "seq"), None),
            P(("fsdp", "seq"), None),
            P(("fsdp", "seq"), None),
            P(("fsdp", "seq"), None),
            P(("fsdp", "seq"), None),
            P(("fsdp", "seq"), None),
            P(("fsdp", "seq")),
            P(("fsdp", "seq")),
            P(("fsdp", "seq")),
            P("seq", None),
        ),
        out_specs=(
            P("fsdp", "seq", None),
            P("fsdp", "seq", None),
            P("fsdp", "seq", None),
            P(("fsdp", "seq"), None),
            P(("fsdp", "seq"), None),
            P(("fsdp", "seq"), None),
            P(("fsdp", "seq"), None),
            P(("fsdp", "seq"), None),
            P(("fsdp", "seq"), None),
            P(("fsdp", "seq"), None),
            P(("fsdp", "seq"), None),
            P(("fsdp", "seq"), None),
            P(("fsdp", "seq"), None),
            P(("fsdp", "seq"), None),
            P(("fsdp", "seq")),
            P(("fsdp", "seq")),
            P(("fsdp", "seq")),
            P("seq", None),
        ),
        check_vma=False,
    )
```

```python
from functools import partial
import math

import jax
import jax.numpy as jnp
from jax import lax
from jax.sharding import PartitionSpec as P

DH = 64
NB = 32


EPS = 1e-06
NEG_LARGE = -1000000000.0
HIGH = lax.Precision.HIGHEST
THRESHOLDS = (19, 21, 24, 27, 31, 35, 40, 46, 52, 59, 67, 77, 87, 99, 113)


def matmul(left, right):
    return jnp.dot(left, right, preferred_element_type=jnp.float32)


def matmul_left_t(left, right):
    return lax.dot_general(
        left, right, (((0,), (0,)), ((), ())), preferred_element_type=jnp.float32
    )


def matmul_right_t(left, right):
    return lax.dot_general(
        left, right, (((1,), (1,)), ((), ())), preferred_element_type=jnp.float32
    )


def bucket_table(query_pos, key_pos):
    distance = jnp.maximum(query_pos[:, None] - key_pos[None, :], 0)
    bucket_ids = jnp.minimum(distance, 16)
    for threshold in THRESHOLDS:
        bucket_ids = bucket_ids + (distance >= threshold).astype(jnp.int32)
    return (bucket_ids[None] == jnp.arange(NB)[:, None, None]).astype(jnp.float32)


def norm_forward(values, gain_vec):
    scale = lax.rsqrt(jnp.mean(values * values, axis=-1, keepdims=True) + EPS)
    unit = values * scale
    return ((unit * gain_vec).astype(jnp.bfloat16), unit, scale)


def norm_backward(grad_normed, unit, scale, gain_vec):
    grad_unit = grad_normed * gain_vec
    grad_gain = jnp.sum(grad_normed * unit, axis=0)
    grad_values = scale * (grad_unit - unit * jnp.mean(grad_unit * unit, axis=-1, keepdims=True))
    return (grad_values, grad_gain)


def attn_scores(queries, key_rows, allowed, pos_bias):
    scores = (
        jnp.einsum("bqhd,bkhd->bhqk", queries, key_rows, preferred_element_type=jnp.float32)
        + pos_bias
    )
    return jnp.where(allowed[:, None], scores, NEG_LARGE)


def attn_forward(queries, key_rows, value_rows, allowed, pos_bias):
    scores = attn_scores(queries, key_rows, allowed, pos_bias)
    top_score = jnp.max(scores, axis=-1, keepdims=True)
    expo = jnp.exp(scores - top_score)
    total = jnp.sum(expo, axis=-1, keepdims=True)
    attn_probs = (expo / total).astype(jnp.bfloat16)
    mixed = jnp.einsum(
        "bhqk,bkhd->bqhd", attn_probs, value_rows, preferred_element_type=jnp.float32
    )
    return (mixed, top_score + jnp.log(total))


def attn_query_side(queries, key_rows, value_rows, allowed, pos_bias, log_total, grad_mixed):
    scores = attn_scores(queries, key_rows, allowed, pos_bias)
    attn_probs = jnp.exp(scores - log_total)
    grad_probs = jnp.einsum(
        "bqhd,bkhd->bhqk", grad_mixed, value_rows, preferred_element_type=jnp.float32
    )
    row_stat = jnp.sum(grad_probs * attn_probs, axis=-1, keepdims=True)
    grad_scores = attn_probs * (grad_probs - row_stat)
    grad_low = grad_scores.astype(jnp.bfloat16)
    grad_query = jnp.einsum(
        "bhqk,bkhd->bqhd", grad_low, key_rows, preferred_element_type=jnp.float32
    )
    return (grad_query, grad_low, attn_probs, row_stat)


def attn_backward(queries, key_rows, value_rows, allowed, pos_bias, log_total, grad_mixed):
    grad_query, grad_low, attn_probs, row_stat = attn_query_side(
        queries, key_rows, value_rows, allowed, pos_bias, log_total, grad_mixed
    )
    grad_key = jnp.einsum("bhqk,bqhd->bkhd", grad_low, queries, preferred_element_type=jnp.float32)
    grad_value = jnp.einsum(
        "bhqk,bqhd->bkhd",
        attn_probs.astype(jnp.bfloat16),
        grad_mixed,
        preferred_element_type=jnp.float32,
    )
    return (grad_query, grad_key, grad_value, grad_low)


def per_device(
    hidden_in,
    encoder_states,
    dec_segments,
    enc_segments,
    cotangent,
    self_query,
    self_key,
    self_value,
    self_output,
    cross_query,
    cross_key,
    cross_value,
    cross_output,
    ffn_gate,
    ffn_up,
    ffn_down,
    norm_self,
    norm_cross,
    norm_ffn,
    bias_table,
):
    row_count, local_len, model_width = hidden_in.shape
    enc_local = encoder_states.shape[1]
    seq_size = lax.axis_size("seq")
    full_len = local_len * seq_size
    full_enc = enc_local * seq_size
    head_count = model_width // DH
    tokens = row_count * local_len
    axes = ("fsdp", "seq")
    total_devices = lax.axis_size("fsdp") * seq_size
    shard_rows = self_query.shape[0]
    down_rows, hidden_width = ffn_down.shape[0], ffn_gate.shape[1]
    folds = -(-down_rows // shard_rows)
    down_padded = jnp.pad(ffn_down, ((0, folds * shard_rows - down_rows), (0, 0)))
    gains = jnp.pad(jnp.stack([norm_self, norm_cross, norm_ffn], axis=1), ((0, 0), (0, 125)))
    first_pack = jnp.concatenate([self_query, self_key, self_value, gains], axis=1)
    rest_pack = jnp.concatenate(
        [self_output, cross_query, cross_key, cross_value, cross_output, ffn_gate, ffn_up]
        + [down_padded[i * shard_rows : (i + 1) * shard_rows] for i in range(folds)],
        axis=1,
    )
    first_full = lax.all_gather(first_pack, axes, axis=0, tiled=True)
    w_qkv = first_full[:, : 3 * model_width]
    gain_rows = first_full[:, 3 * model_width : 3 * model_width + 3].astype(jnp.float32)
    g_self, g_cross, g_ffn = gain_rows[:, 0], gain_rows[:, 1], gain_rows[:, 2]
    buckets_local = bias_table.shape[0]
    bias_high = bias_table.astype(jnp.bfloat16)
    bias_low = (bias_table - bias_high.astype(jnp.float32)).astype(jnp.bfloat16)
    bias_size = buckets_local * head_count
    side_parts = jnp.concatenate(
        [
            dec_segments.astype(jnp.bfloat16),
            enc_segments.astype(jnp.bfloat16),
            jnp.broadcast_to(bias_high.reshape(1, bias_size), (row_count, bias_size)),
            jnp.broadcast_to(bias_low.reshape(1, bias_size), (row_count, bias_size)),
        ],
        axis=1,
    )
    side_pad = jnp.pad(side_parts, ((0, 0), (0, model_width - side_parts.shape[1])))
    side_block = jnp.pad(side_pad[:, None, :], ((0, 0), (0, 15), (0, 0)))
    states_pack = jnp.concatenate([encoder_states, side_block], axis=1)
    states_gathered = lax.all_gather(states_pack, "seq", axis=1, tiled=False)
    states_full = states_gathered[:, :, :enc_local].reshape(row_count, full_enc, model_width)
    side_full = states_gathered[:, :, enc_local].astype(jnp.float32)
    seg_rows = side_full[:, :, :local_len].reshape(row_count, full_len).astype(jnp.int32)
    side_at = local_len + enc_local
    enc_rows = side_full[:, :, local_len:side_at].reshape(row_count, full_enc).astype(jnp.int32)
    table_full = (
        side_full[0, :, side_at : side_at + bias_size]
        + side_full[0, :, side_at + bias_size : side_at + 2 * bias_size]
    ).reshape(seq_size * buckets_local, head_count)
    rest_full = lax.all_gather(rest_pack, axes, axis=0, tiled=True)
    cuts = [model_width] * 5 + [hidden_width] * 2
    pieces, at = [], 0
    for width in cuts:
        pieces.append(rest_full[:, at : at + width])
        at += width
    w_out_self, c_query_w, c_key_w, c_value_w, c_out_w, f_gate, f_up = pieces
    f_down = jnp.concatenate(
        [
            rest_full[:, at + i * model_width : at + (i + 1) * model_width].reshape(
                total_devices, shard_rows, model_width
            )[:, : min(shard_rows, down_rows - i * shard_rows)]
            for i in range(folds)
        ],
        axis=1,
    ).reshape(total_devices * down_rows, model_width)
    query_pos = lax.axis_index("seq") * local_len + jnp.arange(local_len)
    key_pos = jnp.arange(full_len)
    one_hot = bucket_table(query_pos, key_pos)
    pos_bias = jnp.einsum("nqk,nh->hqk", one_hot, table_full, precision=HIGH)
    causal = query_pos[:, None] >= key_pos[None, :]
    block_rows = math.gcd(row_count, max(1, 512 // local_len))
    blocks = row_count // block_rows

    def to_blocks(array_in):
        return array_in.reshape((blocks, block_rows) + array_in.shape[1:])

    x_flat = hidden_in.reshape(tokens, model_width).astype(jnp.float32)
    normed_self, unit_self, scale_self = norm_forward(x_flat, g_self)
    qkv_self = matmul(normed_self, w_qkv).astype(jnp.bfloat16)
    query_self = qkv_self[:, :model_width]
    key_self = qkv_self[:, model_width : 2 * model_width]
    value_self = qkv_self[:, 2 * model_width :]
    pair_self = jnp.stack([key_self, value_self]).reshape(2, row_count, local_len, model_width)
    pair_full = lax.all_gather(pair_self, "seq", axis=2, tiled=True)
    keys_full = pair_full[0].reshape(row_count, full_len, head_count, DH)
    values_full = pair_full[1].reshape(row_count, full_len, head_count, DH)
    queries_heads = query_self.reshape(row_count, local_len, head_count, DH)
    self_allowed = causal[None] & (dec_segments[:, :, None] == seg_rows[:, None, :])

    def self_forward(block_items):
        block_query, block_key, block_value, block_allowed = block_items
        return attn_forward(block_query, block_key, block_value, block_allowed, pos_bias)

    mixed_self, lse_self = lax.map(
        self_forward,
        (
            to_blocks(queries_heads),
            to_blocks(keys_full),
            to_blocks(values_full),
            to_blocks(self_allowed),
        ),
    )
    attn_self = mixed_self.reshape(tokens, model_width).astype(jnp.bfloat16)
    after_self = x_flat + matmul(attn_self, w_out_self)
    normed_cross, unit_cross, scale_cross = norm_forward(after_self, g_cross)
    query_cross = matmul(normed_cross, c_query_w).astype(jnp.bfloat16)
    states_flat = states_full.reshape(row_count * full_enc, model_width)
    key_cross = (
        matmul(states_flat, c_key_w)
        .astype(jnp.bfloat16)
        .reshape(row_count, full_enc, head_count, DH)
    )
    value_cross = (
        matmul(states_flat, c_value_w)
        .astype(jnp.bfloat16)
        .reshape(row_count, full_enc, head_count, DH)
    )
    cross_heads = query_cross.reshape(row_count, local_len, head_count, DH)
    cross_allowed = dec_segments[:, :, None] == enc_rows[:, None, :]

    def cross_forward(block_items):
        block_query, block_key, block_value, block_allowed = block_items
        return attn_forward(block_query, block_key, block_value, block_allowed, 0.0)

    mixed_cross, lse_cross = lax.map(
        cross_forward,
        (
            to_blocks(cross_heads),
            to_blocks(key_cross),
            to_blocks(value_cross),
            to_blocks(cross_allowed),
        ),
    )
    attn_cross = mixed_cross.reshape(tokens, model_width).astype(jnp.bfloat16)
    after_cross = after_self + matmul(attn_cross, c_out_w)
    normed_ffn, unit_ffn, scale_ffn = norm_forward(after_cross, g_ffn)
    gate_pre = matmul(normed_ffn, f_gate)
    up_pre = matmul(normed_ffn, f_up)
    gate_act = jax.nn.gelu(gate_pre, approximate=True)
    hidden_units = (gate_act * up_pre).astype(jnp.bfloat16)
    layer_out = after_cross + matmul(hidden_units, f_down)
    grad_top = cotangent.reshape(tokens, model_width).astype(jnp.float32)
    grad_top_low = grad_top.astype(jnp.bfloat16)
    grad_down_w = matmul_left_t(hidden_units, grad_top_low)
    grad_hidden = matmul_right_t(grad_top_low, f_down)
    gelu_value, gelu_pull = jax.vjp(partial(jax.nn.gelu, approximate=True), gate_pre)
    grad_gate = gelu_pull(grad_hidden * up_pre)[0].astype(jnp.bfloat16)
    grad_up = (grad_hidden * gate_act).astype(jnp.bfloat16)
    grad_gate_w = matmul_left_t(normed_ffn, grad_gate)
    grad_up_w = matmul_left_t(normed_ffn, grad_up)
    down_split = grad_down_w.astype(jnp.bfloat16).reshape(total_devices, down_rows, model_width)
    down_split = jnp.pad(down_split, ((0, 0), (0, folds * shard_rows - down_rows), (0, 0)))
    ffn_pack = jnp.concatenate(
        [grad_gate_w.astype(jnp.bfloat16), grad_up_w.astype(jnp.bfloat16)]
        + [
            down_split[:, i * shard_rows : (i + 1) * shard_rows].reshape(model_width, model_width)
            for i in range(folds)
        ],
        axis=1,
    )
    grad_normed_ffn = matmul_right_t(grad_gate, f_gate) + matmul_right_t(grad_up, f_up)
    grad_res_ffn, grad_g_ffn = norm_backward(grad_normed_ffn, unit_ffn, scale_ffn, g_ffn)
    grad_after_cross = grad_top + grad_res_ffn
    grad_cross_low = grad_after_cross.astype(jnp.bfloat16)
    grad_c_out = matmul_left_t(attn_cross, grad_cross_low)
    grad_attn_cross = (
        matmul_right_t(grad_cross_low, c_out_w)
        .astype(jnp.bfloat16)
        .reshape(row_count, local_len, head_count, DH)
    )

    def cross_back(block_items):
        block_query, block_key, block_value, block_allowed, block_lse, block_grad = block_items
        grad_query, grad_key, grad_value, grad_low = attn_backward(
            block_query, block_key, block_value, block_allowed, 0.0, block_lse, block_grad
        )
        return (grad_query, grad_key, grad_value)

    grad_qc, grad_kc, grad_vc = lax.map(
        cross_back,
        (
            to_blocks(cross_heads),
            to_blocks(key_cross),
            to_blocks(value_cross),
            to_blocks(cross_allowed),
            lse_cross,
            to_blocks(grad_attn_cross),
        ),
    )
    grad_pair_cross = jnp.stack(
        [
            grad_kc.reshape(row_count, full_enc, model_width),
            grad_vc.reshape(row_count, full_enc, model_width),
        ]
    )
    summed_cross = lax.psum_scatter(
        grad_pair_cross.astype(jnp.bfloat16), "seq", scatter_dimension=2, tiled=True
    ).astype(jnp.float32)
    grad_kc_low = summed_cross[0].reshape(row_count * enc_local, model_width).astype(jnp.bfloat16)
    grad_vc_low = summed_cross[1].reshape(row_count * enc_local, model_width).astype(jnp.bfloat16)
    states_local = encoder_states.reshape(row_count * enc_local, model_width)
    grad_c_key = matmul_left_t(states_local, grad_kc_low)
    grad_c_value = matmul_left_t(states_local, grad_vc_low)
    grad_states = matmul_right_t(grad_kc_low, c_key_w) + matmul_right_t(grad_vc_low, c_value_w)
    grad_qc_low = grad_qc.reshape(tokens, model_width).astype(jnp.bfloat16)
    grad_c_query = matmul_left_t(normed_cross, grad_qc_low)
    grad_normed_cross = matmul_right_t(grad_qc_low, c_query_w)
    grad_res_cross, grad_g_cross = norm_backward(
        grad_normed_cross, unit_cross, scale_cross, g_cross
    )
    grad_after_self = grad_after_cross + grad_res_cross
    grad_self_low = grad_after_self.astype(jnp.bfloat16)
    grad_out_self_w = matmul_left_t(attn_self, grad_self_low)
    grad_attn_self = (
        matmul_right_t(grad_self_low, w_out_self)
        .astype(jnp.bfloat16)
        .reshape(row_count, local_len, head_count, DH)
    )

    def self_back(block_items):
        block_query, block_key, block_value, block_allowed, block_lse, block_grad = block_items
        grad_query, grad_key, grad_value, grad_low = attn_backward(
            block_query, block_key, block_value, block_allowed, pos_bias, block_lse, block_grad
        )
        bias_part = jnp.einsum(
            "hqk,nqk->nh", jnp.sum(grad_low.astype(jnp.float32), axis=0), one_hot, precision=HIGH
        )
        return (grad_query, grad_key, grad_value, bias_part)

    grad_qs, grad_ks, grad_vs, bias_parts = lax.map(
        self_back,
        (
            to_blocks(queries_heads),
            to_blocks(keys_full),
            to_blocks(values_full),
            to_blocks(self_allowed),
            lse_self,
            to_blocks(grad_attn_self),
        ),
    )
    grad_pair_self = jnp.stack(
        [
            grad_ks.reshape(row_count, full_len, model_width),
            grad_vs.reshape(row_count, full_len, model_width),
        ]
    )
    summed_self = lax.psum_scatter(
        grad_pair_self.astype(jnp.bfloat16), "seq", scatter_dimension=2, tiled=True
    ).astype(jnp.float32)
    grad_key_low = summed_self[0].reshape(tokens, model_width).astype(jnp.bfloat16)
    grad_value_low = summed_self[1].reshape(tokens, model_width).astype(jnp.bfloat16)
    grad_query_low = grad_qs.reshape(tokens, model_width).astype(jnp.bfloat16)
    grad_q_w = matmul_left_t(normed_self, grad_query_low)
    grad_k_w = matmul_left_t(normed_self, grad_key_low)
    grad_v_w = matmul_left_t(normed_self, grad_value_low)
    grad_normed_self = matmul_right_t(
        jnp.concatenate([grad_query_low, grad_key_low, grad_value_low], axis=1), w_qkv
    )
    grad_res_self, grad_g_self = norm_backward(grad_normed_self, unit_self, scale_self, g_self)
    grad_input = grad_after_self + grad_res_self
    bias_total = jnp.sum(bias_parts, axis=0)
    bias_columns = -(-bias_size // shard_rows)
    bias_spread = jnp.pad(
        bias_total.reshape(seq_size, bias_size),
        ((0, 0), (0, bias_columns * shard_rows - bias_size)),
    ).reshape(1, seq_size * shard_rows, bias_columns)
    fsdp_size = lax.axis_size("fsdp")
    bias_spread = jnp.broadcast_to(
        bias_spread, (fsdp_size, seq_size * shard_rows, bias_columns)
    ).reshape(model_width, bias_columns)
    small = jnp.concatenate(
        [jnp.stack([grad_g_self, grad_g_cross, grad_g_ffn], axis=1), bias_spread], axis=1
    )
    small = jnp.pad(small, ((0, 0), (0, 256 - small.shape[1])))
    late_pack = jnp.concatenate(
        [
            part.astype(jnp.bfloat16)
            for part in (
                grad_q_w,
                grad_k_w,
                grad_v_w,
                grad_out_self_w,
                grad_c_query,
                grad_c_key,
                grad_c_value,
                grad_c_out,
                small,
            )
        ],
        axis=1,
    )
    whole_pack = jnp.concatenate([ffn_pack, late_pack], axis=1)
    whole_summed = lax.psum_scatter(whole_pack, axes, scatter_dimension=0, tiled=True)
    whole_summed = whole_summed.astype(jnp.float32)
    ffn_summed = whole_summed[:, : ffn_pack.shape[1]]
    late_summed = whole_summed[:, ffn_pack.shape[1] :]
    down_share = jnp.concatenate(
        [
            ffn_summed[:, 2 * hidden_width + i * model_width :][:, :model_width]
            for i in range(folds)
        ],
        axis=0,
    )[:down_rows]
    small_summed = late_summed[:, 8 * model_width :]
    bias_sum = small_summed[:, 3 : 3 + bias_columns].reshape(-1)[:bias_size]
    bias_grad = bias_sum.reshape(buckets_local, head_count)
    grads_sharded = (
        *(late_summed[:, i * model_width : (i + 1) * model_width] for i in range(8)),
        ffn_summed[:, :hidden_width],
        ffn_summed[:, hidden_width : 2 * hidden_width],
        down_share,
        small_summed[:, 0],
        small_summed[:, 1],
        small_summed[:, 2],
    )
    return (
        layer_out.reshape(row_count, local_len, model_width).astype(jnp.bfloat16),
        grad_input.reshape(row_count, local_len, model_width).astype(jnp.bfloat16),
        grad_states.reshape(row_count, enc_local, model_width).astype(jnp.bfloat16),
        grads_sharded[0],
        grads_sharded[1],
        grads_sharded[2],
        grads_sharded[3],
        grads_sharded[4],
        grads_sharded[5],
        grads_sharded[6],
        grads_sharded[7],
        grads_sharded[8],
        grads_sharded[9],
        grads_sharded[10],
        grads_sharded[11],
        grads_sharded[12],
        grads_sharded[13],
        bias_grad,
    )


def solution(mesh):
    return jax.shard_map(
        per_device,
        mesh=mesh,
        in_specs=(
            P("fsdp", "seq", None),
            P("fsdp", "seq", None),
            P("fsdp", "seq"),
            P("fsdp", "seq"),
            P("fsdp", "seq", None),
            P(("fsdp", "seq"), None),
            P(("fsdp", "seq"), None),
            P(("fsdp", "seq"), None),
            P(("fsdp", "seq"), None),
            P(("fsdp", "seq"), None),
            P(("fsdp", "seq"), None),
            P(("fsdp", "seq"), None),
            P(("fsdp", "seq"), None),
            P(("fsdp", "seq"), None),
            P(("fsdp", "seq"), None),
            P(("fsdp", "seq"), None),
            P(("fsdp", "seq")),
            P(("fsdp", "seq")),
            P(("fsdp", "seq")),
            P("seq", None),
        ),
        out_specs=(
            P("fsdp", "seq", None),
            P("fsdp", "seq", None),
            P("fsdp", "seq", None),
            P(("fsdp", "seq"), None),
            P(("fsdp", "seq"), None),
            P(("fsdp", "seq"), None),
            P(("fsdp", "seq"), None),
            P(("fsdp", "seq"), None),
            P(("fsdp", "seq"), None),
            P(("fsdp", "seq"), None),
            P(("fsdp", "seq"), None),
            P(("fsdp", "seq"), None),
            P(("fsdp", "seq"), None),
            P(("fsdp", "seq"), None),
            P(("fsdp", "seq")),
            P(("fsdp", "seq")),
            P(("fsdp", "seq")),
            P("seq", None),
        ),
        check_vma=False,
    )
```
